32 devices in a mesh: member: 2 (over x), pts: 4 (over y, core), sub: 4 (over z).
Axes of the slice: x: 2, y: 2, z: 4, core: 2. Of those that a mesh axis runs over, the one named last changes fastest.
Arguments:
- spectra: float32 [2592, 4, 512], P('member', 'sub', 'pts'), parts along dimension 0, may hold values from 0.2 to 2
- sea_mask: int32 [4, 512], P('sub', 'pts'), may hold values 0 or 1
- wind_speed: float32 [8, 512], P(('member', 'sub'), 'pts'), parts along dimension 0, may hold values from 0.5 to 2
- growth: float32 [1296], replicated, may hold values from 0.02 to 0.2
- damping: float32 [1296], replicated, may hold values from 0.02 to 0.2
- quartets: int32 [1296, 4], replicated, may hold values from 0 to 1295
- coupling: float32 [1296], replicated, may hold values from 0.05 to 0.3
- upwind: int32 [2, 36, 4, 512], P(None, None, 'sub'), may hold values from 0 to 2
- courant: float32 [2, 1296], replicated, may hold values from 0.1 to 0.9
- obs_point: int32 [4096], replicated, may hold values from 0 to 2047
- obs_hs: float32 [4096], replicated, may hold values from 90 to 170
- nearest: int32 [4, 512], P('sub', 'pts'), may hold values from 0 to 4095
Outputs:
- analysis: float32 [2592, 4, 512], P('member', 'sub', 'pts'), parts along dimension 0
- track_heights: float32 [8192], P('member'), parts along dimension 0
The draws below stay inside these ranges and needn't reach their ends.
There are 2 independent parts, one for each index of `member`. The reference program is written for one: setup_inputs(seed, part) draws one part's arguments, and reference() takes and returns one part's arrays. A program takes and returns all parts, laid end to end along the dimension named above; an argument that names none is the same for every part. Nothing has to cross between parts.
All inputs are finite; a program needn't handle non-finite values. No bound on the sum of `sea_mask` on one device may be relied on, other than what follows from the above.
Results may differ from the reference program's by a relative error of at most 0.0001.
Values sent between devices are 32-bit elements; how exact they have to be, the bound alone decides.
A program may use at most 64 MiB of HBM per device.

```python
import math
import jax
import jax.numpy as jnp
from jax import lax

NF = 36
ND = 36
NOBS = 4096
STEPS = 2
NB = 1296
NQ = 1296
NX = 4
NY = 512


def place_ends(values, rng, least, largest):
    longest = values.shape.index(max(values.shape))
    spots = []
    for shift in (0, 1):
        where = [jax.random.randint(jax.random.fold_in(rng, axis), (), 0, length) for axis, length in enumerate(values.shape)]
        where[longest] = (where[longest] + shift) % values.shape[longest]
        spots.append(tuple(where))
    return values.at[spots[0]].set(least).at[spots[1]].set(largest)


def steps_of(stream_key, dims, cuts, smallest, top_value):
    level, own = 1.0, jax.random.fold_in(stream_key, 6)
    for dim, shards_of in cuts:
        steps = jnp.exp(jax.random.uniform(jax.random.fold_in(own, dim), (shards_of,), jnp.float32, smallest / len(cuts), top_value / len(cuts)))
        level = level * jnp.repeat(steps, dims[dim] // shards_of).reshape([-1 if axis == dim else 1 for axis in range(len(dims))])
    return level


def setup_inputs(seed: int = 0, part: int = 0) -> dict:
    seeds = jax.random.split(jax.random.key(seed), 13)
    part_keys = jax.random.split(jax.random.fold_in(seeds[12], part), 13)
    return {
        "spectra": jnp.clip(jnp.exp(math.log(2.0) - 2.3025851 * jax.random.uniform(part_keys[0], (NB, NX, NY), jnp.float32) ** steps_of(part_keys[0], (NB, NX, NY), ((1, 4), (2, 4)), -0.2, 0.2)), 0.2, 2.0),
        "sea_mask": place_ends((jax.random.randint(seeds[1], (NX, NY), 0, 4) < 3).astype(jnp.int32), jax.random.fold_in(seeds[1], 1), 0, 1),
        "wind_speed": jnp.clip(0.5 + 1.5 * jax.random.uniform(part_keys[2], (NX, NY), jnp.float32) ** steps_of(part_keys[2], (NX, NY), ((0, 4), (1, 4)), -0.2, 0.2), 0.5, 2.0),
        "growth": jnp.clip(jnp.exp(jax.random.uniform(seeds[3], (NB,), jnp.float32, math.log(0.02), math.log(0.2))), 0.02, 0.2),
        "damping": jnp.clip(jnp.exp(jax.random.uniform(seeds[4], (NB,), jnp.float32, math.log(0.02), math.log(0.2))), 0.02, 0.2),
        "quartets": place_ends(jax.random.randint(seeds[5], (NQ, 4), 0, NB), jax.random.fold_in(seeds[5], 1), 0, NB - 1).astype(jnp.int32),
        "coupling": jnp.clip(jnp.exp(jax.random.uniform(seeds[6], (NQ,), jnp.float32, math.log(0.05), math.log(0.3))), 0.05, 0.3),
        "upwind": place_ends(jax.random.randint(seeds[7], (2, ND, NX, NY), 0, 3), jax.random.fold_in(seeds[7], 1), 0, 2).astype(jnp.int32),
        "courant": jnp.clip(jax.random.uniform(seeds[8], (2, NB), jnp.float32, 0.1, 0.9), 0.1, 0.9),
        "obs_point": place_ends(jax.random.randint(seeds[9], (NOBS,), 0, NX * NY), jax.random.fold_in(seeds[9], 1), 0, (NX * NY) - 1).astype(jnp.int32),
        "obs_hs": jnp.clip(jax.random.uniform(seeds[10], (NOBS,), jnp.float32, 90.0, 170.0), 90.0, 170.0),
        "nearest": place_ends(jax.random.randint(seeds[11], (NX, NY), 0, NOBS), jax.random.fold_in(seeds[11], 1), 0, NOBS - 1).astype(jnp.int32),
    }


obs_gain = 0.6

def interact(row_values, quartets, coupling):
    shaped_coupling = coupling.reshape((-1,) + (1,) * (row_values.ndim - 1))
    bin_one = row_values[quartets[:, 0]]
    bin_two = row_values[quartets[:, 1]]
    bin_three = row_values[quartets[:, 2]]
    bin_four = row_values[quartets[:, 3]]
    flux_term = shaped_coupling * (bin_one * bin_two * (bin_three + bin_four) - bin_three * bin_four * (bin_one + bin_two))
    nonlinear = jnp.zeros_like(row_values)
    nonlinear = nonlinear.at[quartets[:, 0]].add(-flux_term)
    nonlinear = nonlinear.at[quartets[:, 1]].add(-flux_term)
    nonlinear = nonlinear.at[quartets[:, 2]].add(flux_term)
    nonlinear = nonlinear.at[quartets[:, 3]].add(flux_term)
    return nonlinear

def source_terms(spectrum, sea_mask, wind_speed, growth, damping, quartets, coupling):
    masked = spectrum * sea_mask.astype(jnp.float32)[None]
    mean_energy = lax.optimization_barrier(jnp.sum(masked, axis=0)) / masked.shape[0]
    growth_rate = growth[:, None, None] * wind_speed[None] - damping[:, None, None] * mean_energy[None]
    grown_spec = masked * jnp.exp(growth_rate)
    by_rows = lax.map(lambda row_values: interact(row_values, quartets, coupling), jnp.moveaxis(masked, 1, 0))
    nonlinear = jnp.moveaxis(by_rows, 0, 1)
    return jnp.maximum(grown_spec + nonlinear, 0.1 * grown_spec)

def advect(spectrum, upwind, courant):
    blocked = spectrum.reshape(NF, ND, NX, NY)
    lon_code = upwind[0][None]
    lat_code = upwind[1][None]
    courant_lon = courant[0].reshape(NF, ND, 1, 1)
    courant_lat = courant[1].reshape(NF, ND, 1, 1)
    from_west = jnp.roll(blocked, 1, axis=3)
    from_east = jnp.roll(blocked, -1, axis=3)
    upstream = jnp.where(lon_code == 0, from_west, jnp.where(lon_code == 2, from_east, blocked))
    blocked = blocked - courant_lon * (blocked - upstream)
    padded = jnp.pad(blocked, ((0, 0), (0, 0), (1, 1), (0, 0)))
    upstream = jnp.where(lat_code == 0, padded[:, :, :-2], jnp.where(lat_code == 2, padded[:, :, 2:], blocked))
    blocked = blocked - courant_lat * (blocked - upstream)
    return blocked.reshape(NF * ND, NX, NY)

def reference(spectra, sea_mask, wind_speed, growth, damping, quartets, coupling, upwind, courant, obs_point, obs_hs, nearest):
    spectrum = spectra
    for iteration in range(STEPS):
        spectrum = source_terms(spectrum, sea_mask, wind_speed, growth, damping, quartets, coupling)
        spectrum = advect(spectrum, upwind, courant)
    masked = spectrum * sea_mask.astype(jnp.float32)[None]
    energy = lax.optimization_barrier(jnp.sum(masked, axis=0))
    wave_height = 4.0 * jnp.sqrt(energy)
    track_heights = wave_height.reshape(-1)[obs_point]
    innovation = obs_hs - track_heights
    target = wave_height + obs_gain * innovation[nearest]
    scale_ratio = (jnp.maximum(target, 0.5 * wave_height) / (wave_height + 1e-06)) ** 2
    return (masked * scale_ratio[None], track_heights)
```

```python
import functools

import jax
import jax.numpy as jnp
from jax import lax
from jax.experimental import pallas as pl
from jax.experimental.pallas import tpu as pltpu
from jax.sharding import PartitionSpec as P

ND = 36
STEPS = 2
LANES = 128
TILE = 2 * ND
OBS_GAIN = 0.6
MESH = pl.DeviceIdType.MESH
EXACT = lax.Precision.HIGHEST


def row_chunks(total, width):
    starts = list(range(0, total - width + 1, width))
    ends = starts[1:] + [total]
    return tuple((s, e - s) for s, e in zip(starts, ends))


def block_rows(total, most):
    best = 16
    for rows in range(16, most + 1, 16):
        if total % rows == 0:
            best = rows
    return best


def halves(value):
    high = value.astype(jnp.bfloat16)
    low = (value - high.astype(jnp.float32)).astype(jnp.bfloat16)
    return high, low


def thirds(value):
    first = value.astype(jnp.bfloat16)
    rest = value - first.astype(jnp.float32)
    second, third = halves(rest)
    return first, second, third


def one_hot_rows(index_row, height):
    rows = lax.broadcasted_iota(jnp.int32, (height, index_row.shape[1]), 0)
    return jnp.where(rows == index_row, 1.0, 0.0)


def table_pick(table, picks, row_row):
    first, second, third = thirds(table)
    by_lane = (
        jnp.dot(first, picks, preferred_element_type=jnp.float32)
        + jnp.dot(second, picks, preferred_element_type=jnp.float32)
        + jnp.dot(third, picks, preferred_element_type=jnp.float32)
    )
    chosen = one_hot_rows(row_row, table.shape[0])
    return jnp.sum(by_lane * chosen, axis=0, keepdims=True)


def kernel(
    pts_total,
    sub_total,
    chunks,
    quad_block,
    spec_ref,
    mask_ref,
    wind_ref,
    cols_ref,
    quad_ref,
    quad_t_ref,
    codes_ref,
    obs_row_ref,
    obs_table_ref,
    hs_table_ref,
    near_ref,
    out_ref,
    track_ref,
    picks,
    signs,
    gathered,
    split_values,
    split_flux,
    masked_ref,
    sourced,
    advected,
    lower,
    higher,
    lon_codes,
    lat_codes,
    edge_out,
    edge_in,
    obs_picks,
    heights,
    west_send,
    west_recv,
    east_send,
    east_recv,
    up_send,
    up_recv,
    down_send,
    down_recv,
    height_send,
    height_recv,
):
    member = lax.axis_index("member")
    my_pts = lax.axis_index("pts")
    my_sub = lax.axis_index("sub")
    peers = pts_total * sub_total
    me = my_sub * pts_total + my_pts
    west = (member, lax.rem(my_pts + pts_total - 1, pts_total), my_sub)
    east = (member, lax.rem(my_pts + 1, pts_total), my_sub)
    above = (member, my_pts, my_sub + 1)
    below = (member, my_pts, my_sub - 1)
    has_above = my_sub < sub_total - 1
    has_below = my_sub > 0
    bins = spec_ref.shape[0]
    quads = quad_ref.shape[0]
    quad_blocks = quads // quad_block

    def peer_id(offset):
        peer = lax.rem(me + offset, peers)
        return peer, (member, lax.rem(peer, pts_total), lax.div(peer, pts_total))

    barrier = pltpu.get_barrier_semaphore()

    @pl.loop(1, peers)
    def _(offset):
        pl.semaphore_signal(barrier, inc=1, device_id=peer_id(offset)[1], device_id_type=MESH)

    mask = mask_ref[...].astype(jnp.float32)
    wind = wind_ref[...]

    def take_chunk(value, start, size):
        value = value * mask
        masked_ref[pl.ds(start, size), :] = value
        high, low = halves(value)
        split_values[pl.ds(start, size), :LANES] = high
        split_values[pl.ds(start, size), LANES:] = low
        return jnp.sum(value, axis=0, keepdims=True)

    energy = jnp.zeros((1, LANES), jnp.float32)
    for start, size in chunks:
        energy = energy + take_chunk(spec_ref[pl.ds(start, size), :], start, size)

    part = 48 if quad_block % 48 == 0 else 16

    @pl.loop(0, quad_blocks)
    def _(block):
        for member_of_quad in range(4):
            @pl.loop(0, quad_block // part)
            def _(inner):
                row = pl.multiple_of(block * quad_block + inner * part, part)
                index = quad_ref[pl.ds(row, part), member_of_quad : member_of_quad + 1]
                lanes = lax.broadcasted_iota(jnp.int32, (part, bins), 1)
                hot = jnp.where(lanes == index, 1.0, 0.0).astype(jnp.bfloat16)
                to = pl.multiple_of(
                    block * (4 * quad_block) + member_of_quad * quad_block + inner * part, part
                )
                picks[pl.ds(to, part), :] = hot

    part_b = 48 if bins % 48 == 0 else 16

    @pl.loop(0, bins // part_b)
    def _(block):
        row = pl.multiple_of(block * part_b, part_b)
        rows = lax.broadcasted_iota(jnp.int32, (part_b, quads), 0) + row
        total = jnp.zeros((part_b, quads), jnp.float32)
        for member_of_quad, sign in enumerate((-1.0, -1.0, 1.0, 1.0)):
            index = quad_t_ref[member_of_quad : member_of_quad + 1, :]
            total = total + jnp.where(rows == index, sign, 0.0)
        signs[pl.ds(row, part_b), :] = total.astype(jnp.bfloat16)

    @pl.loop(0, bins // TILE)
    def _(block):
        row = pl.multiple_of(block * TILE, TILE)
        lon_codes[pl.ds(row, TILE), :] = codes_ref[0]
        lat_codes[pl.ds(row, TILE), :] = codes_ref[1]

    @pl.when(jnp.logical_not(has_below))
    def _():
        lower[...] = jnp.zeros_like(lower)

    @pl.when(jnp.logical_not(has_above))
    def _():
        higher[...] = jnp.zeros_like(higher)

    def gather_block(block, start, size):
        rows = pl.ds(pl.multiple_of(block * (4 * quad_block), 4 * quad_block), 4 * quad_block)
        got = jnp.dot(
            picks[rows, pl.ds(start, size)],
            split_values[pl.ds(start, size), :],
            preferred_element_type=jnp.float32,
        )
        return rows, got[:, :LANES] + got[:, LANES:]

    def flux_block(block, got):
        rows = pl.ds(pl.multiple_of(block * quad_block, quad_block), quad_block)
        one, two, three, four = (got[k * quad_block : (k + 1) * quad_block] for k in range(4))
        weight = cols_ref[rows, 4:5]
        flux = weight * (one * two * (three + four) - three * four * (one + two))
        high, low = halves(flux)
        split_flux[rows, :LANES] = high
        split_flux[rows, LANES:] = low

    lane = lax.broadcasted_iota(jnp.int32, (1, LANES), 1)
    sel_row = lax.broadcasted_iota(jnp.int32, (8, LANES), 0)
    sel_lane = lax.broadcasted_iota(jnp.int32, (8, LANES), 1)
    edge_select = jnp.where(
        ((sel_row == 0) & (sel_lane == 0)) | ((sel_row == 1) & (sel_lane == LANES - 1)), 1.0, 0.0
    )
    put_row = lax.broadcasted_iota(jnp.int32, (16, LANES), 0)
    put_lane = lax.broadcasted_iota(jnp.int32, (16, LANES), 1)
    edge_place = jnp.where(
        ((put_row == 1) & (put_lane == 0)) | ((put_row == 8) & (put_lane == LANES - 1)), 1.0, 0.0
    )

    def edge_copies(step, c):
        to_west = pltpu.make_async_remote_copy(
            src_ref=edge_out.at[step, c],
            dst_ref=edge_in.at[step, c, 1],
            send_sem=west_send.at[step, c],
            recv_sem=west_recv.at[step, c],
            device_id=west,
            device_id_type=MESH,
        )
        to_east = pltpu.make_async_remote_copy(
            src_ref=edge_out.at[step, c],
            dst_ref=edge_in.at[step, c, 0],
            send_sem=east_send.at[step, c],
            recv_sem=east_recv.at[step, c],
            device_id=east,
            device_id_type=MESH,
        )
        return to_west, to_east

    def row_copies(step, c):
        start, size = chunks[c]
        rows = pl.ds(start, size)
        to_above = pltpu.make_async_remote_copy(
            src_ref=advected.at[step, rows],
            dst_ref=lower.at[step, rows],
            send_sem=up_send.at[step, c],
            recv_sem=up_recv.at[step, c],
            device_id=above,
            device_id_type=MESH,
        )
        to_below = pltpu.make_async_remote_copy(
            src_ref=advected.at[step, rows],
            dst_ref=higher.at[step, rows],
            send_sem=down_send.at[step, c],
            recv_sem=down_recv.at[step, c],
            device_id=below,
            device_id_type=MESH,
        )
        return to_above, to_below

    def source_chunk(step, c, mean):
        start, size = chunks[c]
        rows = pl.ds(start, size)
        change = jnp.dot(signs[rows, :], split_flux[...], preferred_element_type=jnp.float32)
        change = change[:, :LANES] + change[:, LANES:]
        rate = cols_ref[rows, 0:1] * wind - cols_ref[rows, 1:2] * mean
        grown = masked_ref[rows, :] * jnp.exp(rate)
        value = jnp.maximum(grown + change, 0.1 * grown)
        sourced[rows, :] = value
        edge_out[step, c, :, :size] = lax.dot_general(
            edge_select,
            value,
            (((1,), (1,)), ((), ())),
            precision=EXACT,
            preferred_element_type=jnp.float32,
        )
        for copy in edge_copies(step, c):
            copy.start()

    def lon_chunk(step, c):
        start, size = chunks[c]
        rows = pl.ds(start, size)
        to_west, to_east = edge_copies(step, c)
        to_west.wait_recv()
        to_east.wait_recv()
        edges = jnp.concatenate([edge_in[step, c, 0, :, :size], edge_in[step, c, 1, :, :size]], axis=0)
        outside = lax.dot_general(
            edges,
            edge_place,
            (((0,), (0,)), ((), ())),
            precision=EXACT,
            preferred_element_type=jnp.float32,
        )
        value = sourced[rows, :]
        from_west = jnp.where(lane == 0, outside, pltpu.roll(value, 1, 1))
        from_east = jnp.where(lane == LANES - 1, outside, pltpu.roll(value, LANES - 1, 1))
        code = lon_codes[rows, :]
        upstream = jnp.where(code == 0, from_west, jnp.where(code == 2, from_east, value))
        advected[step, rows, :] = value - cols_ref[rows, 2:3] * (value - upstream)
        to_above, to_below = row_copies(step, c)

        @pl.when(has_above)
        def _():
            to_above.start()

        @pl.when(has_below)
        def _():
            to_below.start()

    def lat_chunk(step, c):
        start, size = chunks[c]
        rows = pl.ds(start, size)
        to_above, to_below = row_copies(step, c)

        @pl.when(has_below)
        def _():
            to_above.wait_recv()

        @pl.when(has_above)
        def _():
            to_below.wait_recv()

        value = advected[step, rows, :]
        code = lat_codes[rows, :]
        upstream = jnp.where(
            code == 0, lower[step, rows, :], jnp.where(code == 2, higher[step, rows, :], value)
        )
        return value - cols_ref[rows, 3:4] * (value - upstream)

    def source_and_lon(step, mean):
        for c in range(len(chunks)):
            source_chunk(step, c, mean)
            if c > 0:
                lon_chunk(step, c - 1)
        lon_chunk(step, len(chunks) - 1)

    @pl.loop(0, quad_blocks)
    def _(block):
        flux_block(block, gather_block(block, 0, bins)[1])

    pl.semaphore_wait(barrier, peers - 1)
    source_and_lon(0, energy / bins)

    obs_point = obs_row_ref[...]
    obs_picks[...] = one_hot_rows(lax.rem(obs_point, LANES), LANES).astype(jnp.bfloat16)
    near = near_ref[...]
    near_picks = one_hot_rows(lax.rem(near, LANES), LANES).astype(jnp.bfloat16)
    near_row = lax.div(near, LANES)
    near_hs = table_pick(hs_table_ref[...], near_picks, near_row)
    near_point = table_pick(obs_table_ref[...].astype(jnp.float32), near_picks, near_row)

    for step in range(1, STEPS):
        energy = jnp.zeros((1, LANES), jnp.float32)
        for c, (start, size) in enumerate(chunks):
            energy = energy + take_chunk(lat_chunk(step - 1, c), start, size)

            @pl.loop(0, quad_blocks)
            def _(block):
                rows, got = gather_block(block, start, size)
                if c > 0:
                    got = gathered[rows, :] + got
                if c < len(chunks) - 1:
                    gathered[rows, :] = got
                else:
                    flux_block(block, got)

        source_and_lon(step, energy / bins)

    energy = jnp.zeros((1, LANES), jnp.float32)
    for c, (start, size) in enumerate(chunks):
        value = lat_chunk(STEPS - 1, c) * mask
        masked_ref[pl.ds(start, size), :] = value
        energy = energy + jnp.sum(value, axis=0, keepdims=True)
    wave_height = 4.0 * jnp.sqrt(energy)
    heights[me] = jnp.broadcast_to(wave_height, (8, LANES))

    def height_copy(slot, to):
        return pltpu.make_async_remote_copy(
            src_ref=heights.at[me],
            dst_ref=heights.at[me],
            send_sem=height_send.at[slot],
            recv_sem=height_recv.at[me],
            device_id=to,
            device_id_type=MESH,
        )

    @pl.loop(1, peers)
    def _(offset):
        height_copy(offset, peer_id(offset)[1]).start()

    @pl.loop(1, peers)
    def _(offset):
        peer, to = peer_id(offset)
        pltpu.make_async_remote_copy(
            src_ref=heights.at[me],
            dst_ref=heights.at[peer],
            send_sem=height_send.at[offset],
            recv_sem=height_recv.at[peer],
            device_id=to,
            device_id_type=MESH,
        ).wait_recv()

    table = heights[:, 0, :]
    track = table_pick(table, obs_picks[...], lax.div(obs_point, LANES))
    track_ref[...] = track
    near_point = near_point.astype(jnp.int32)
    near_lane = one_hot_rows(lax.rem(near_point, LANES), LANES).astype(jnp.bfloat16)
    near_track = table_pick(table, near_lane, lax.div(near_point, LANES))
    target = wave_height + OBS_GAIN * (near_hs - near_track)
    ratio = jnp.maximum(target, 0.5 * wave_height) / (wave_height + 1e-6)
    scale = ratio * ratio
    for start, size in chunks:
        out_ref[pl.ds(start, size), :] = masked_ref[pl.ds(start, size), :] * scale

    for step in range(STEPS):
        for c in range(len(chunks)):
            for copy in edge_copies(step, c):
                copy.wait_send()
            to_above, to_below = row_copies(step, c)

            @pl.when(has_above)
            def _():
                to_above.wait_send()

            @pl.when(has_below)
            def _():
                to_below.wait_send()

    @pl.loop(1, peers)
    def _(offset):
        height_copy(offset, peer_id(offset)[1]).wait_send()


def body(
    pts_total,
    sub_total,
    spectra,
    sea_mask,
    wind_speed,
    growth,
    damping,
    quartets,
    coupling,
    upwind,
    courant,
    obs_point,
    obs_hs,
    nearest,
):
    bins = spectra.shape[0]
    quads = quartets.shape[0]
    observations = obs_point.shape[0]
    chunks = row_chunks(bins, 256)
    most = max(size for _, size in chunks)
    wide = -(-most // LANES) * LANES
    quad_block = block_rows(quads, 432)
    peers = pts_total * sub_total
    cols = jnp.stack([growth, damping, courant[0], courant[1], coupling], axis=1)
    codes = lax.dynamic_slice_in_dim(upwind, lax.axis_index("pts") * LANES, LANES, 3)[:, :, 0]
    codes = jnp.concatenate([codes, codes], axis=1)
    f32, bf16 = jnp.float32, jnp.bfloat16
    count = len(chunks)
    vmem = pl.BlockSpec(memory_space=pltpu.VMEM)
    analysis, track = pl.pallas_call(
        functools.partial(kernel, pts_total, sub_total, chunks, quad_block),
        out_shape=(
            jax.ShapeDtypeStruct((bins, LANES), f32),
            jax.ShapeDtypeStruct((1, observations), f32),
        ),
        in_specs=[vmem] * 11,
        out_specs=(vmem, vmem),
        scratch_shapes=[
            pltpu.VMEM((4 * quads, bins), bf16),
            pltpu.VMEM((bins, quads), bf16),
            pltpu.VMEM((4 * quads, LANES), f32),
            pltpu.VMEM((bins, 2 * LANES), bf16),
            pltpu.VMEM((quads, 2 * LANES), bf16),
            pltpu.VMEM((bins, LANES), f32),
            pltpu.VMEM((bins, LANES), f32),
            pltpu.VMEM((STEPS, bins, LANES), f32),
            pltpu.VMEM((STEPS, bins, LANES), f32),
            pltpu.VMEM((STEPS, bins, LANES), f32),
            pltpu.VMEM((bins, LANES), jnp.int32),
            pltpu.VMEM((bins, LANES), jnp.int32),
            pltpu.VMEM((STEPS, count, 8, wide), f32),
            pltpu.VMEM((STEPS, count, 2, 8, wide), f32),
            pltpu.VMEM((LANES, observations), bf16),
            pltpu.VMEM((peers, 8, LANES), f32),
        ]
        + [pltpu.SemaphoreType.DMA((STEPS, count))] * 8
        + [pltpu.SemaphoreType.DMA((peers,))] * 2,
        compiler_params=pltpu.CompilerParams(
            collective_id=0, has_side_effects=True, vmem_limit_bytes=56 * 1024 * 1024
        ),
    )(
        spectra.reshape(bins, LANES),
        sea_mask,
        wind_speed,
        cols,
        quartets,
        quartets.T,
        codes,
        obs_point.reshape(1, observations),
        obs_point.reshape(-1, LANES),
        obs_hs.reshape(-1, LANES),
        nearest,
    )
    return analysis.reshape(bins, 1, LANES), track.reshape(observations)


def solution(mesh):
    in_specs = (
        P("member", "sub", "pts"),
        P("sub", "pts"),
        P(("member", "sub"), "pts"),
        P(),
        P(),
        P(),
        P(),
        P(None, None, "sub", None),
        P(),
        P(),
        P(),
        P("sub", "pts"),
    )
    out_specs = (P("member", "sub", "pts"), P("member"))
    return jax.shard_map(
        functools.partial(body, mesh.shape["pts"], mesh.shape["sub"]),
        mesh=mesh,
        in_specs=in_specs,
        out_specs=out_specs,
        check_vma=False,
    )
```

```python
import functools

import jax
import jax.numpy as jnp
from jax import lax
from jax.experimental import pallas as pl
from jax.experimental.pallas import tpu as pltpu
from jax.sharding import PartitionSpec as P

ND = 36
STEPS = 2
LANES = 128
TILE = 2 * ND
LAG = 2
OBS_GAIN = 0.6
MESH = pl.DeviceIdType.MESH


def row_chunks(total, width):
    starts = list(range(0, total - width + 1, width))
    ends = starts[1:] + [total]
    return tuple((s, e - s) for s, e in zip(starts, ends))


def block_rows(total, most):
    best = 16
    for rows in range(16, most + 1, 16):
        if total % rows == 0:
            best = rows
    return best


def halves(value):
    high = value.astype(jnp.bfloat16)
    low = (value - high.astype(jnp.float32)).astype(jnp.bfloat16)
    return high, low


def thirds(value):
    first = value.astype(jnp.bfloat16)
    rest = value - first.astype(jnp.float32)
    second, third = halves(rest)
    return first, second, third


def one_hot_rows(index_row, height):
    rows = lax.broadcasted_iota(jnp.int32, (height, index_row.shape[1]), 0)
    return jnp.where(rows == index_row, 1.0, 0.0)


def table_pick(table, picks, row_row):
    first, second, third = thirds(table)
    by_lane = (
        jnp.dot(first, picks, preferred_element_type=jnp.float32)
        + jnp.dot(second, picks, preferred_element_type=jnp.float32)
        + jnp.dot(third, picks, preferred_element_type=jnp.float32)
    )
    chosen = one_hot_rows(row_row, table.shape[0])
    return jnp.sum(by_lane * chosen, axis=0, keepdims=True)


def kernel(
    pts_total,
    sub_total,
    chunks,
    quad_block,
    spec_ref,
    mask_ref,
    wind_ref,
    growth_ref,
    damping_ref,
    courant_ref,
    coupling_ref,
    quad_t_ref,
    codes_in_ref,
    obs_row_ref,
    obs_table_ref,
    hs_table_ref,
    near_ref,
    masked_ref,
    track_ref,
    scale_ref,
    picks,
    signs,
    gathered,
    split_values,
    split_flux,
    sourced,
    advected,
    lower,
    higher,
    lon_codes,
    lat_codes,
    edge_out,
    edge_in,
    obs_picks,
    heights,
    cols_ref,
    quad_ref,
    codes_ref,
    turn,
    west_send,
    west_recv,
    east_send,
    east_recv,
    up_send,
    up_recv,
    down_send,
    down_recv,
    height_send,
    height_recv,
):
    member = lax.axis_index("member")
    my_pts = lax.axis_index("pts")
    my_sub = lax.axis_index("sub")
    peers = pts_total * sub_total
    me = my_sub * pts_total + my_pts
    west = (member, lax.rem(my_pts + pts_total - 1, pts_total), my_sub)
    east = (member, lax.rem(my_pts + 1, pts_total), my_sub)
    above = (member, my_pts, my_sub + 1)
    below = (member, my_pts, my_sub - 1)
    has_above = my_sub < sub_total - 1
    has_below = my_sub > 0
    bins = spec_ref.shape[0]
    quads = quad_t_ref.shape[1]
    quad_blocks = quads // quad_block

    def peer_id(offset):
        peer = lax.rem(me + offset, peers)
        return peer, (member, lax.rem(peer, pts_total), lax.div(peer, pts_total))

    barrier = pltpu.get_barrier_semaphore()

    @pl.loop(1, peers)
    def _(offset):
        pl.semaphore_signal(barrier, inc=1, device_id=peer_id(offset)[1], device_id_type=MESH)

    turn[...] = jnp.zeros_like(turn)
    turn[0:4, :quads] = quad_t_ref[...].astype(jnp.float32)
    quad_ref[...] = turn[...].T[:quads].astype(jnp.int32)
    turn[0, :bins] = growth_ref[...]
    turn[1, :bins] = damping_ref[...]
    turn[2:4, :bins] = courant_ref[...]
    turn[4, :quads] = coupling_ref[...]
    cols_ref[...] = turn[...].T[:bins]
    for axis in range(2):
        mine = codes_in_ref[pl.ds(axis * ND * pts_total + my_pts, ND, stride=pts_total), :]
        codes_ref[axis, :ND] = mine
        codes_ref[axis, ND:] = mine

    mask = mask_ref[...].astype(jnp.float32)
    wind = wind_ref[...]

    def take_chunk(value, start, size):
        value = value * mask
        masked_ref[pl.ds(start, size), :] = value
        high, low = halves(value)
        split_values[pl.ds(start, size), :LANES] = high
        split_values[pl.ds(start, size), LANES:] = low
        return jnp.sum(value, axis=0, keepdims=True)

    energy = jnp.zeros((1, LANES), jnp.float32)
    for start, size in chunks:
        energy = energy + take_chunk(spec_ref[pl.ds(start, size), :], start, size)

    one16 = jnp.bfloat16(1)
    zero16 = jnp.bfloat16(0)

    @pl.loop(0, quad_blocks)
    def _(block):
        for member_of_quad in range(4):
            row = pl.multiple_of(block * quad_block, quad_block)
            index = quad_ref[pl.ds(row, quad_block), member_of_quad : member_of_quad + 1]
            lanes = lax.broadcasted_iota(jnp.int32, (quad_block, bins), 1).astype(jnp.int16)
            index = jnp.broadcast_to(index, (quad_block, LANES)).astype(jnp.int16)
            index = jnp.concatenate([index] * (-(-bins // LANES)), axis=1)[:, :bins]
            to = pl.multiple_of(block * (4 * quad_block) + member_of_quad * quad_block, quad_block)
            picks[pl.ds(to, quad_block), :] = jnp.where(lanes == index, one16, zero16)

    def sign_rows(row, size):
        rows = (lax.broadcasted_iota(jnp.int32, (size, quads), 0) + row).astype(jnp.int16)
        total = None
        for member_of_quad, sign in enumerate((-one16, -one16, one16, one16)):
            index = jnp.broadcast_to(quad_t_ref[member_of_quad : member_of_quad + 1, :], (16, quads))
            index = jnp.concatenate([index.astype(jnp.int16)] * (size // 16), axis=0)
            term = jnp.where(rows == index, sign, zero16)
            total = term if total is None else total + term
        signs[pl.ds(row, size), :] = total

    @pl.loop(0, bins // TILE)
    def _(block):
        row = pl.multiple_of(block * TILE, TILE)
        lon_codes[pl.ds(row, TILE), :] = codes_ref[0]
        lat_codes[pl.ds(row, TILE), :] = codes_ref[1]

    @pl.when(jnp.logical_not(has_below))
    def _():
        lower[...] = jnp.zeros_like(lower)

    @pl.when(jnp.logical_not(has_above))
    def _():
        higher[...] = jnp.zeros_like(higher)

    def gather_block(block, start, size):
        rows = pl.ds(pl.multiple_of(block * (4 * quad_block), 4 * quad_block), 4 * quad_block)
        got = jnp.dot(
            picks[rows, pl.ds(start, size)],
            split_values[pl.ds(start, size), :],
            preferred_element_type=jnp.float32,
        )
        return rows, got[:, :LANES] + got[:, LANES:]

    def flux_block(block, got):
        rows = pl.ds(pl.multiple_of(block * quad_block, quad_block), quad_block)
        one, two, three, four = (got[k * quad_block : (k + 1) * quad_block] for k in range(4))
        weight = cols_ref[rows, 4:5]
        flux = weight * (one * two * (three + four) - three * four * (one + two))
        high, low = halves(flux)
        split_flux[rows, :LANES] = high
        split_flux[rows, LANES:] = low

    lane = lax.broadcasted_iota(jnp.int32, (1, LANES), 1)
    sel_row = lax.broadcasted_iota(jnp.int32, (8, 2 * LANES), 0)
    sel_lane = lax.rem(lax.broadcasted_iota(jnp.int32, (8, 2 * LANES), 1), LANES)
    edge_select = jnp.where(
        ((sel_row == 0) & (sel_lane == 0)) | ((sel_row == 1) & (sel_lane == LANES - 1)), 1.0, 0.0
    ).astype(jnp.bfloat16)
    put_row = lax.rem(lax.broadcasted_iota(jnp.int32, (32, LANES), 0), 16)
    put_lane = lax.broadcasted_iota(jnp.int32, (32, LANES), 1)
    edge_place = jnp.where(
        ((put_row == 1) & (put_lane == 0)) | ((put_row == 8) & (put_lane == LANES - 1)), 1.0, 0.0
    ).astype(jnp.bfloat16)

    def edge_copies(step, c):
        to_west = pltpu.make_async_remote_copy(
            src_ref=edge_out.at[step, c],
            dst_ref=edge_in.at[step, c, 1],
            send_sem=west_send.at[step, c],
            recv_sem=west_recv.at[step, c],
            device_id=west,
            device_id_type=MESH,
        )
        to_east = pltpu.make_async_remote_copy(
            src_ref=edge_out.at[step, c],
            dst_ref=edge_in.at[step, c, 0],
            send_sem=east_send.at[step, c],
            recv_sem=east_recv.at[step, c],
            device_id=east,
            device_id_type=MESH,
        )
        return to_west, to_east

    def row_copies(step, c):
        start, size = chunks[c]
        rows = pl.ds(start, size)
        to_above = pltpu.make_async_remote_copy(
            src_ref=advected.at[step, rows],
            dst_ref=lower.at[step, rows],
            send_sem=up_send.at[step, c],
            recv_sem=up_recv.at[step, c],
            device_id=above,
            device_id_type=MESH,
        )
        to_below = pltpu.make_async_remote_copy(
            src_ref=advected.at[step, rows],
            dst_ref=higher.at[step, rows],
            send_sem=down_send.at[step, c],
            recv_sem=down_recv.at[step, c],
            device_id=below,
            device_id_type=MESH,
        )
        return to_above, to_below

    def source_chunk(step, c, mean):
        start, size = chunks[c]
        rows = pl.ds(start, size)
        change = sourced[rows, :]
        rate = cols_ref[rows, 0:1] * wind - cols_ref[rows, 1:2] * mean
        grown = masked_ref[rows, :] * jnp.exp(rate)
        value = jnp.maximum(grown + change, 0.1 * grown)
        sourced[rows, :] = value
        edge_out[step, c, :, :size] = lax.dot_general(
            edge_select,
            jnp.concatenate(halves(value), axis=1),
            (((1,), (1,)), ((), ())),
            preferred_element_type=jnp.float32,
        )
        for copy in edge_copies(step, c):
            copy.start()

    def lon_chunk(step, c):
        start, size = chunks[c]
        rows = pl.ds(start, size)
        to_west, to_east = edge_copies(step, c)
        to_west.wait_recv()
        to_east.wait_recv()
        edges = jnp.concatenate([edge_in[step, c, 0, :, :size], edge_in[step, c, 1, :, :size]], axis=0)
        outside = lax.dot_general(
            jnp.concatenate(halves(edges), axis=0),
            edge_place,
            (((0,), (0,)), ((), ())),
            preferred_element_type=jnp.float32,
        )
        value = sourced[rows, :]
        from_west = jnp.where(lane == 0, outside, pltpu.roll(value, 1, 1))
        from_east = jnp.where(lane == LANES - 1, outside, pltpu.roll(value, LANES - 1, 1))
        code = lon_codes[rows, :]
        upstream = jnp.where(code == 0, from_west, jnp.where(code == 2, from_east, value))
        advected[step, rows, :] = value - cols_ref[rows, 2:3] * (value - upstream)
        to_above, to_below = row_copies(step, c)

        @pl.when(has_above)
        def _():
            to_above.start()

        @pl.when(has_below)
        def _():
            to_below.start()

    def lat_chunk(step, c):
        start, size = chunks[c]
        rows = pl.ds(start, size)
        to_above, to_below = row_copies(step, c)

        @pl.when(has_below)
        def _():
            to_above.wait_recv()

        @pl.when(has_above)
        def _():
            to_below.wait_recv()

        value = advected[step, rows, :]
        code = lat_codes[rows, :]
        upstream = jnp.where(
            code == 0, lower[step, rows, :], jnp.where(code == 2, higher[step, rows, :], value)
        )
        return value - cols_ref[rows, 3:4] * (value - upstream)

    def source_and_lon(step, mean):
        change = jnp.dot(signs[...], split_flux[...], preferred_element_type=jnp.float32)
        sourced[...] = change[:, :LANES] + change[:, LANES:]
        for c in range(len(chunks) + LAG):
            if c < len(chunks):
                source_chunk(step, c, mean)
            if c >= LAG:
                lon_chunk(step, c - LAG)

    sign_part = block_rows(bins // quad_blocks, 144)

    @pl.loop(0, quad_blocks)
    def _(block):
        flux_block(block, gather_block(block, 0, bins)[1])
        for piece in range(bins // quad_blocks // sign_part):
            row = block * (bins // quad_blocks) + piece * sign_part
            sign_rows(pl.multiple_of(row, sign_part), sign_part)

    pl.semaphore_wait(barrier, peers - 1)
    source_and_lon(0, energy / bins)

    obs_point = obs_row_ref[...]
    obs_picks[...] = one_hot_rows(lax.rem(obs_point, LANES), LANES).astype(jnp.bfloat16)
    near = near_ref[...]
    near_picks = one_hot_rows(lax.rem(near, LANES), LANES).astype(jnp.bfloat16)
    near_row = lax.div(near, LANES)
    near_hs = table_pick(hs_table_ref[...], near_picks, near_row)
    near_point = table_pick(obs_table_ref[...].astype(jnp.float32), near_picks, near_row)

    for step in range(1, STEPS):
        energy = jnp.zeros((1, LANES), jnp.float32)
        for c, (start, size) in enumerate(chunks):
            energy = energy + take_chunk(lat_chunk(step - 1, c), start, size)

            @pl.loop(0, quad_blocks)
            def _(block):
                rows, got = gather_block(block, start, size)
                if c > 0:
                    got = gathered[rows, :] + got
                if c < len(chunks) - 1:
                    gathered[rows, :] = got
                else:
                    flux_block(block, got)

        source_and_lon(step, energy / bins)

    energy = jnp.zeros((1, LANES), jnp.float32)
    for c, (start, size) in enumerate(chunks):
        value = lat_chunk(STEPS - 1, c) * mask
        masked_ref[pl.ds(start, size), :] = value
        energy = energy + jnp.sum(value, axis=0, keepdims=True)
    wave_height = 4.0 * jnp.sqrt(energy)
    heights[me] = jnp.broadcast_to(wave_height, (8, LANES))

    def height_copy(slot, to):
        return pltpu.make_async_remote_copy(
            src_ref=heights.at[me],
            dst_ref=heights.at[me],
            send_sem=height_send.at[slot],
            recv_sem=height_recv.at[me],
            device_id=to,
            device_id_type=MESH,
        )

    @pl.loop(1, peers)
    def _(offset):
        height_copy(offset, peer_id(offset)[1]).start()

    @pl.loop(1, peers)
    def _(offset):
        peer, to = peer_id(offset)
        pltpu.make_async_remote_copy(
            src_ref=heights.at[me],
            dst_ref=heights.at[peer],
            send_sem=height_send.at[offset],
            recv_sem=height_recv.at[peer],
            device_id=to,
            device_id_type=MESH,
        ).wait_recv()

    table = heights[:, 0, :]
    track = table_pick(table, obs_picks[...], lax.div(obs_point, LANES))
    track_ref[...] = track
    near_point = near_point.astype(jnp.int32)
    near_lane = one_hot_rows(lax.rem(near_point, LANES), LANES).astype(jnp.bfloat16)
    near_track = table_pick(table, near_lane, lax.div(near_point, LANES))
    target = wave_height + OBS_GAIN * (near_hs - near_track)
    ratio = jnp.maximum(target, 0.5 * wave_height) / (wave_height + 1e-6)
    scale_ref[...] = ratio * ratio

    for step in range(STEPS):
        for c in range(len(chunks)):
            for copy in edge_copies(step, c):
                copy.wait_send()
            to_above, to_below = row_copies(step, c)

            @pl.when(has_above)
            def _():
                to_above.wait_send()

            @pl.when(has_below)
            def _():
                to_below.wait_send()

    @pl.loop(1, peers)
    def _(offset):
        height_copy(offset, peer_id(offset)[1]).wait_send()


def finish(masked_ref, track_in, scale_ref, out_ref, track_out):
    out_ref[...] = masked_ref[...] * scale_ref[...]
    track_out[...] = track_in[...]


def body(
    pts_total,
    sub_total,
    spectra,
    sea_mask,
    wind_speed,
    growth,
    damping,
    quartets,
    coupling,
    upwind,
    courant,
    obs_point,
    obs_hs,
    nearest,
):
    bins = spectra.shape[0]
    quads = quartets.shape[0]
    observations = obs_point.shape[0]
    chunks = row_chunks(bins, 256)
    most = max(size for _, size in chunks)
    wide = -(-most // LANES) * LANES
    quad_block = block_rows(quads, 432)
    peers = pts_total * sub_total
    f32, bf16 = jnp.float32, jnp.bfloat16
    count = len(chunks)
    vmem = pl.BlockSpec(memory_space=pltpu.VMEM)
    masked, track, scale = pl.pallas_call(
        functools.partial(kernel, pts_total, sub_total, chunks, quad_block),
        out_shape=(
            jax.ShapeDtypeStruct((bins, LANES), f32),
            jax.ShapeDtypeStruct((1, observations), f32),
            jax.ShapeDtypeStruct((1, LANES), f32),
        ),
        in_specs=[vmem] * 13,
        out_specs=(vmem, vmem, vmem),
        scratch_shapes=[
            pltpu.VMEM((4 * quads, bins), bf16),
            pltpu.VMEM((bins, quads), bf16),
            pltpu.VMEM((4 * quads, LANES), f32),
            pltpu.VMEM((bins, 2 * LANES), bf16),
            pltpu.VMEM((quads, 2 * LANES), bf16),
            pltpu.VMEM((bins, LANES), f32),
            pltpu.VMEM((STEPS, bins, LANES), f32),
            pltpu.VMEM((STEPS, bins, LANES), f32),
            pltpu.VMEM((STEPS, bins, LANES), f32),
            pltpu.VMEM((bins, LANES), jnp.int32),
            pltpu.VMEM((bins, LANES), jnp.int32),
            pltpu.VMEM((STEPS, count, 8, wide), f32),
            pltpu.VMEM((STEPS, count, 2, 8, wide), f32),
            pltpu.VMEM((LANES, observations), bf16),
            pltpu.VMEM((peers, 8, LANES), f32),
            pltpu.VMEM((bins, 8), f32),
            pltpu.VMEM((quads, 8), jnp.int32),
            pltpu.VMEM((2, TILE, LANES), jnp.int32),
            pltpu.VMEM((8, -(-max(bins, quads) // LANES) * LANES), f32),
        ]
        + [pltpu.SemaphoreType.DMA((STEPS, count))] * 8
        + [pltpu.SemaphoreType.DMA((peers,))] * 2,
        compiler_params=pltpu.CompilerParams(
            collective_id=0, has_side_effects=True, vmem_limit_bytes=56 * 1024 * 1024
        ),
    )(
        spectra.reshape(bins, LANES),
        sea_mask,
        wind_speed,
        growth,
        damping,
        courant,
        coupling,
        quartets.T,
        upwind.reshape(-1, LANES),
        obs_point.reshape(1, observations),
        obs_point.reshape(-1, LANES),
        obs_hs.reshape(-1, LANES),
        nearest,
    )
    analysis, track = pl.pallas_call(
        finish,
        out_shape=(
            jax.ShapeDtypeStruct((bins, LANES), f32),
            jax.ShapeDtypeStruct((1, observations), f32),
        ),
        in_specs=[vmem] * 3,
        out_specs=(vmem, vmem),
        compiler_params=pltpu.CompilerParams(vmem_limit_bytes=8 * 1024 * 1024),
    )(masked, track, scale)
    return analysis.reshape(bins, 1, LANES), track.reshape(observations)


def solution(mesh):
    in_specs = (
        P("member", "sub", "pts"),
        P("sub", "pts"),
        P(("member", "sub"), "pts"),
        P(),
        P(),
        P(),
        P(),
        P(None, None, "sub", None),
        P(),
        P(),
        P(),
        P("sub", "pts"),
    )
    out_specs = (P("member", "sub", "pts"), P("member"))
    return jax.shard_map(
        functools.partial(body, mesh.shape["pts"], mesh.shape["sub"]),
        mesh=mesh,
        in_specs=in_specs,
        out_specs=out_specs,
        check_vma=False,
    )
```

```python
import functools

import jax
import jax.numpy as jnp
from jax import lax
from jax.experimental import pallas as pl
from jax.experimental.pallas import tpu as pltpu
from jax.sharding import PartitionSpec as P

ND = 36
STEPS = 2
LANES = 128
TILE = 2 * ND
LAG = 2
OBS_GAIN = 0.6
MESH = pl.DeviceIdType.MESH


def row_chunks(total, width):
    starts = list(range(0, total - width + 1, width))
    ends = starts[1:] + [total]
    return tuple((s, e - s) for s, e in zip(starts, ends))


def block_rows(total, most):
    best = 16
    for rows in range(16, most + 1, 16):
        if total % rows == 0:
            best = rows
    return best


def halves(value):
    high = value.astype(jnp.bfloat16)
    low = (value - high.astype(jnp.float32)).astype(jnp.bfloat16)
    return high, low


def thirds(value):
    first = value.astype(jnp.bfloat16)
    rest = value - first.astype(jnp.float32)
    second, third = halves(rest)
    return first, second, third


def one_hot_rows(index_row, height):
    rows = lax.broadcasted_iota(jnp.int32, (height, index_row.shape[1]), 0)
    return jnp.where(rows == index_row, 1.0, 0.0)


def table_pick(table, picks, row_row):
    first, second, third = thirds(table)
    by_lane = (
        jnp.dot(first, picks, preferred_element_type=jnp.float32)
        + jnp.dot(second, picks, preferred_element_type=jnp.float32)
        + jnp.dot(third, picks, preferred_element_type=jnp.float32)
    )
    chosen = one_hot_rows(row_row, table.shape[0])
    return jnp.sum(by_lane * chosen, axis=0, keepdims=True)


def kernel(
    pts_total,
    sub_total,
    chunks,
    quad_block,
    spec_ref,
    mask_ref,
    wind_ref,
    growth_ref,
    damping_ref,
    courant_ref,
    coupling_ref,
    quad_t_ref,
    codes_in_ref,
    obs_row_ref,
    obs_table_ref,
    hs_table_ref,
    near_ref,
    masked_ref,
    track_ref,
    scale_ref,
    picks,
    signs,
    gathered,
    split_values,
    split_flux,
    sourced,
    advected,
    lower,
    higher,
    lon_codes,
    lat_codes,
    edge_out,
    edge_in,
    obs_picks,
    heights,
    cols_ref,
    quad_ref,
    codes_ref,
    turn,
    west_send,
    west_recv,
    east_send,
    east_recv,
    up_send,
    up_recv,
    down_send,
    down_recv,
    height_send,
    height_recv,
):
    member = lax.axis_index("member")
    my_pts = lax.axis_index("pts")
    my_sub = lax.axis_index("sub")
    peers = pts_total * sub_total
    me = my_sub * pts_total + my_pts
    west = (member, lax.rem(my_pts + pts_total - 1, pts_total), my_sub)
    east = (member, lax.rem(my_pts + 1, pts_total), my_sub)
    above = (member, my_pts, my_sub + 1)
    below = (member, my_pts, my_sub - 1)
    has_above = my_sub < sub_total - 1
    has_below = my_sub > 0
    bins = spec_ref.shape[0]
    quads = quad_t_ref.shape[1]
    quad_blocks = quads // quad_block

    def peer_id(offset):
        peer = lax.rem(me + offset, peers)
        return peer, (member, lax.rem(peer, pts_total), lax.div(peer, pts_total))

    barrier = pltpu.get_barrier_semaphore()

    @pl.loop(1, peers)
    def _(offset):
        pl.semaphore_signal(barrier, inc=1, device_id=peer_id(offset)[1], device_id_type=MESH)

    turn[...] = jnp.zeros_like(turn)
    turn[0:4, :quads] = quad_t_ref[...].astype(jnp.float32)
    quad_ref[...] = turn[...].T[:quads].astype(jnp.int32)
    turn[0, :bins] = growth_ref[...]
    turn[1, :bins] = damping_ref[...]
    turn[2:4, :bins] = courant_ref[...]
    turn[4, :quads] = coupling_ref[...]
    cols_ref[...] = turn[...].T[:bins]
    for axis in range(2):
        mine = codes_in_ref[pl.ds(axis * ND * pts_total + my_pts, ND, stride=pts_total), :]
        codes_ref[axis, :ND] = mine
        codes_ref[axis, ND:] = mine

    mask = mask_ref[...].astype(jnp.float32)
    wind = wind_ref[...]

    def take_chunk(value, start, size):
        value = value * mask
        masked_ref[pl.ds(start, size), :] = value
        high, low = halves(value)
        split_values[pl.ds(start, size), :LANES] = high
        split_values[pl.ds(start, size), LANES:] = low
        return jnp.sum(value, axis=0, keepdims=True)

    energy = jnp.zeros((1, LANES), jnp.float32)
    for start, size in chunks:
        energy = energy + take_chunk(spec_ref[pl.ds(start, size), :], start, size)

    one16 = jnp.bfloat16(1)
    zero16 = jnp.bfloat16(0)

    def pick_rows(block, member_of_quad):
        row = pl.multiple_of(block * quad_block, quad_block)
        index = quad_ref[pl.ds(row, quad_block), member_of_quad : member_of_quad + 1]
        lanes = lax.broadcasted_iota(jnp.int32, (quad_block, bins), 1).astype(jnp.int16)
        index = jnp.broadcast_to(index, (quad_block, LANES)).astype(jnp.int16)
        index = jnp.concatenate([index] * (-(-bins // LANES)), axis=1)[:, :bins]
        to = pl.multiple_of(block * (4 * quad_block) + member_of_quad * quad_block, quad_block)
        hot = jnp.where(lanes == index, one16, zero16)
        picks[pl.ds(to, quad_block), :] = hot
        got = jnp.dot(hot, split_values[...], preferred_element_type=jnp.float32)
        return got[:, :LANES] + got[:, LANES:]

    def sign_rows(row, size):
        rows = (lax.broadcasted_iota(jnp.int32, (size, quads), 0) + row).astype(jnp.int16)
        total = None
        for member_of_quad, sign in enumerate((-one16, -one16, one16, one16)):
            index = jnp.broadcast_to(quad_t_ref[member_of_quad : member_of_quad + 1, :], (16, quads))
            index = jnp.concatenate([index.astype(jnp.int16)] * (size // 16), axis=0)
            term = jnp.where(rows == index, sign, zero16)
            total = term if total is None else total + term
        signs[pl.ds(row, size), :] = total

    @pl.loop(0, bins // TILE)
    def _(block):
        row = pl.multiple_of(block * TILE, TILE)
        lon_codes[pl.ds(row, TILE), :] = codes_ref[0]
        lat_codes[pl.ds(row, TILE), :] = codes_ref[1]

    @pl.when(jnp.logical_not(has_below))
    def _():
        lower[...] = jnp.zeros_like(lower)

    @pl.when(jnp.logical_not(has_above))
    def _():
        higher[...] = jnp.zeros_like(higher)

    def gather_block(block, start, size):
        rows = pl.ds(pl.multiple_of(block * (4 * quad_block), 4 * quad_block), 4 * quad_block)
        got = jnp.dot(
            picks[rows, pl.ds(start, size)],
            split_values[pl.ds(start, size), :],
            preferred_element_type=jnp.float32,
        )
        return rows, got[:, :LANES] + got[:, LANES:]

    def flux_block(block, got):
        rows = pl.ds(pl.multiple_of(block * quad_block, quad_block), quad_block)
        one, two, three, four = (got[k * quad_block : (k + 1) * quad_block] for k in range(4))
        weight = cols_ref[rows, 4:5]
        flux = weight * (one * two * (three + four) - three * four * (one + two))
        high, low = halves(flux)
        split_flux[rows, :LANES] = high
        split_flux[rows, LANES:] = low

    lane = lax.broadcasted_iota(jnp.int32, (1, LANES), 1)
    sel_row = lax.broadcasted_iota(jnp.int32, (8, 2 * LANES), 0)
    sel_lane = lax.rem(lax.broadcasted_iota(jnp.int32, (8, 2 * LANES), 1), LANES)
    edge_select = jnp.where(
        ((sel_row == 0) & (sel_lane == 0)) | ((sel_row == 1) & (sel_lane == LANES - 1)), 1.0, 0.0
    ).astype(jnp.bfloat16)
    put_row = lax.rem(lax.broadcasted_iota(jnp.int32, (32, LANES), 0), 16)
    put_lane = lax.broadcasted_iota(jnp.int32, (32, LANES), 1)
    edge_place = jnp.where(
        ((put_row == 1) & (put_lane == 0)) | ((put_row == 8) & (put_lane == LANES - 1)), 1.0, 0.0
    ).astype(jnp.bfloat16)

    def edge_copies(step, c):
        to_west = pltpu.make_async_remote_copy(
            src_ref=edge_out.at[step, c],
            dst_ref=edge_in.at[step, c, 1],
            send_sem=west_send.at[step, c],
            recv_sem=west_recv.at[step, c],
            device_id=west,
            device_id_type=MESH,
        )
        to_east = pltpu.make_async_remote_copy(
            src_ref=edge_out.at[step, c],
            dst_ref=edge_in.at[step, c, 0],
            send_sem=east_send.at[step, c],
            recv_sem=east_recv.at[step, c],
            device_id=east,
            device_id_type=MESH,
        )
        return to_west, to_east

    def row_copies(step, c):
        start, size = chunks[c]
        rows = pl.ds(start, size)
        to_above = pltpu.make_async_remote_copy(
            src_ref=advected.at[step, rows],
            dst_ref=lower.at[step, rows],
            send_sem=up_send.at[step, c],
            recv_sem=up_recv.at[step, c],
            device_id=above,
            device_id_type=MESH,
        )
        to_below = pltpu.make_async_remote_copy(
            src_ref=advected.at[step, rows],
            dst_ref=higher.at[step, rows],
            send_sem=down_send.at[step, c],
            recv_sem=down_recv.at[step, c],
            device_id=below,
            device_id_type=MESH,
        )
        return to_above, to_below

    def source_chunk(step, c, mean):
        start, size = chunks[c]
        rows = pl.ds(start, size)
        change = sourced[rows, :]
        rate = cols_ref[rows, 0:1] * wind - cols_ref[rows, 1:2] * mean
        grown = masked_ref[rows, :] * jnp.exp(rate)
        value = jnp.maximum(grown + change, 0.1 * grown)
        sourced[rows, :] = value
        edge_out[step, c, :, :size] = lax.dot_general(
            edge_select,
            jnp.concatenate(halves(value), axis=1),
            (((1,), (1,)), ((), ())),
            preferred_element_type=jnp.float32,
        )
        for copy in edge_copies(step, c):
            copy.start()

    def lon_chunk(step, c):
        start, size = chunks[c]
        rows = pl.ds(start, size)
        to_west, to_east = edge_copies(step, c)
        to_west.wait_recv()
        to_east.wait_recv()
        edges = jnp.concatenate([edge_in[step, c, 0, :, :size], edge_in[step, c, 1, :, :size]], axis=0)
        outside = lax.dot_general(
            jnp.concatenate(halves(edges), axis=0),
            edge_place,
            (((0,), (0,)), ((), ())),
            preferred_element_type=jnp.float32,
        )
        value = sourced[rows, :]
        from_west = jnp.where(lane == 0, outside, pltpu.roll(value, 1, 1))
        from_east = jnp.where(lane == LANES - 1, outside, pltpu.roll(value, LANES - 1, 1))
        code = lon_codes[rows, :]
        upstream = jnp.where(code == 0, from_west, jnp.where(code == 2, from_east, value))
        advected[step, rows, :] = value - cols_ref[rows, 2:3] * (value - upstream)
        to_above, to_below = row_copies(step, c)

        @pl.when(has_above)
        def _():
            to_above.start()

        @pl.when(has_below)
        def _():
            to_below.start()

    def lat_chunk(step, c):
        start, size = chunks[c]
        rows = pl.ds(start, size)
        to_above, to_below = row_copies(step, c)

        @pl.when(has_below)
        def _():
            to_above.wait_recv()

        @pl.when(has_above)
        def _():
            to_below.wait_recv()

        value = advected[step, rows, :]
        code = lat_codes[rows, :]
        upstream = jnp.where(
            code == 0, lower[step, rows, :], jnp.where(code == 2, higher[step, rows, :], value)
        )
        return value - cols_ref[rows, 3:4] * (value - upstream)

    def source_and_lon(step, mean):
        change = jnp.dot(signs[...], split_flux[...], preferred_element_type=jnp.float32)
        sourced[...] = change[:, :LANES] + change[:, LANES:]
        for c in range(len(chunks) + LAG):
            if c < len(chunks):
                source_chunk(step, c, mean)
            if c >= LAG:
                lon_chunk(step, c - LAG)

    sign_part = block_rows(bins // quad_blocks, 144)

    @pl.loop(0, quad_blocks)
    def _(block):
        flux_block(block, jnp.concatenate([pick_rows(block, k) for k in range(4)], axis=0))
        for piece in range(bins // quad_blocks // sign_part):
            row = block * (bins // quad_blocks) + piece * sign_part
            sign_rows(pl.multiple_of(row, sign_part), sign_part)

    pl.semaphore_wait(barrier, peers - 1)
    source_and_lon(0, energy / bins)

    obs_point = obs_row_ref[...]
    obs_picks[...] = one_hot_rows(lax.rem(obs_point, LANES), LANES).astype(jnp.bfloat16)
    near = near_ref[...]
    near_picks = one_hot_rows(lax.rem(near, LANES), LANES).astype(jnp.bfloat16)
    near_row = lax.div(near, LANES)
    near_hs = table_pick(hs_table_ref[...], near_picks, near_row)
    near_point = table_pick(obs_table_ref[...].astype(jnp.float32), near_picks, near_row)

    for step in range(1, STEPS):
        energy = jnp.zeros((1, LANES), jnp.float32)
        for c, (start, size) in enumerate(chunks):
            energy = energy + take_chunk(lat_chunk(step - 1, c), start, size)

            @pl.loop(0, quad_blocks)
            def _(block):
                rows, got = gather_block(block, start, size)
                if c > 0:
                    got = gathered[rows, :] + got
                if c < len(chunks) - 1:
                    gathered[rows, :] = got
                else:
                    flux_block(block, got)

        source_and_lon(step, energy / bins)

    energy = jnp.zeros((1, LANES), jnp.float32)
    for c, (start, size) in enumerate(chunks):
        value = lat_chunk(STEPS - 1, c) * mask
        masked_ref[pl.ds(start, size), :] = value
        energy = energy + jnp.sum(value, axis=0, keepdims=True)
    wave_height = 4.0 * jnp.sqrt(energy)
    heights[me] = jnp.broadcast_to(wave_height, (8, LANES))

    def height_copy(slot, to):
        return pltpu.make_async_remote_copy(
            src_ref=heights.at[me],
            dst_ref=heights.at[me],
            send_sem=height_send.at[slot],
            recv_sem=height_recv.at[me],
            device_id=to,
            device_id_type=MESH,
        )

    @pl.loop(1, peers)
    def _(offset):
        height_copy(offset, peer_id(offset)[1]).start()

    @pl.loop(1, peers)
    def _(offset):
        peer, to = peer_id(offset)
        pltpu.make_async_remote_copy(
            src_ref=heights.at[me],
            dst_ref=heights.at[peer],
            send_sem=height_send.at[offset],
            recv_sem=height_recv.at[peer],
            device_id=to,
            device_id_type=MESH,
        ).wait_recv()

    table = heights[:, 0, :]
    track = table_pick(table, obs_picks[...], lax.div(obs_point, LANES))
    track_ref[...] = track
    near_point = near_point.astype(jnp.int32)
    near_lane = one_hot_rows(lax.rem(near_point, LANES), LANES).astype(jnp.bfloat16)
    near_track = table_pick(table, near_lane, lax.div(near_point, LANES))
    target = wave_height + OBS_GAIN * (near_hs - near_track)
    ratio = jnp.maximum(target, 0.5 * wave_height) / (wave_height + 1e-6)
    scale_ref[...] = ratio * ratio

    for step in range(STEPS):
        for c in range(len(chunks)):
            for copy in edge_copies(step, c):
                copy.wait_send()
            to_above, to_below = row_copies(step, c)

            @pl.when(has_above)
            def _():
                to_above.wait_send()

            @pl.when(has_below)
            def _():
                to_below.wait_send()

    @pl.loop(1, peers)
    def _(offset):
        height_copy(offset, peer_id(offset)[1]).wait_send()


def finish(masked_ref, track_in, scale_ref, out_ref, track_out):
    out_ref[...] = masked_ref[...] * scale_ref[...]
    track_out[...] = track_in[...]


def body(
    pts_total,
    sub_total,
    spectra,
    sea_mask,
    wind_speed,
    growth,
    damping,
    quartets,
    coupling,
    upwind,
    courant,
    obs_point,
    obs_hs,
    nearest,
):
    bins = spectra.shape[0]
    quads = quartets.shape[0]
    observations = obs_point.shape[0]
    chunks = row_chunks(bins, 256)
    most = max(size for _, size in chunks)
    wide = -(-most // LANES) * LANES
    quad_block = block_rows(quads, 432)
    peers = pts_total * sub_total
    f32, bf16 = jnp.float32, jnp.bfloat16
    count = len(chunks)
    vmem = pl.BlockSpec(memory_space=pltpu.VMEM)
    masked, track, scale = pl.pallas_call(
        functools.partial(kernel, pts_total, sub_total, chunks, quad_block),
        out_shape=(
            jax.ShapeDtypeStruct((bins, LANES), f32),
            jax.ShapeDtypeStruct((1, observations), f32),
            jax.ShapeDtypeStruct((1, LANES), f32),
        ),
        in_specs=[vmem] * 13,
        out_specs=(vmem, vmem, vmem),
        scratch_shapes=[
            pltpu.VMEM((4 * quads, bins), bf16),
            pltpu.VMEM((bins, quads), bf16),
            pltpu.VMEM((4 * quads, LANES), f32),
            pltpu.VMEM((bins, 2 * LANES), bf16),
            pltpu.VMEM((quads, 2 * LANES), bf16),
            pltpu.VMEM((bins, LANES), f32),
            pltpu.VMEM((STEPS, bins, LANES), f32),
            pltpu.VMEM((STEPS, bins, LANES), f32),
            pltpu.VMEM((STEPS, bins, LANES), f32),
            pltpu.VMEM((bins, LANES), jnp.int32),
            pltpu.VMEM((bins, LANES), jnp.int32),
            pltpu.VMEM((STEPS, count, 8, wide), f32),
            pltpu.VMEM((STEPS, count, 2, 8, wide), f32),
            pltpu.VMEM((LANES, observations), bf16),
            pltpu.VMEM((peers, 8, LANES), f32),
            pltpu.VMEM((bins, 8), f32),
            pltpu.VMEM((quads, 8), jnp.int32),
            pltpu.VMEM((2, TILE, LANES), jnp.int32),
            pltpu.VMEM((8, -(-max(bins, quads) // LANES) * LANES), f32),
        ]
        + [pltpu.SemaphoreType.DMA((STEPS, count))] * 8
        + [pltpu.SemaphoreType.DMA((peers,))] * 2,
        compiler_params=pltpu.CompilerParams(
            collective_id=0, has_side_effects=True, vmem_limit_bytes=56 * 1024 * 1024
        ),
    )(
        spectra.reshape(bins, LANES),
        sea_mask,
        wind_speed,
        growth,
        damping,
        courant,
        coupling,
        quartets.T,
        upwind.reshape(-1, LANES),
        obs_point.reshape(1, observations),
        obs_point.reshape(-1, LANES),
        obs_hs.reshape(-1, LANES),
        nearest,
    )
    analysis, track = pl.pallas_call(
        finish,
        out_shape=(
            jax.ShapeDtypeStruct((bins, LANES), f32),
            jax.ShapeDtypeStruct((1, observations), f32),
        ),
        in_specs=[vmem] * 3,
        out_specs=(vmem, vmem),
        compiler_params=pltpu.CompilerParams(vmem_limit_bytes=56 * 1024 * 1024),
    )(masked, track, scale)
    return analysis.reshape(bins, 1, LANES), track.reshape(observations)


def solution(mesh):
    in_specs = (
        P("member", "sub", "pts"),
        P("sub", "pts"),
        P(("member", "sub"), "pts"),
        P(),
        P(),
        P(),
        P(),
        P(None, None, "sub", None),
        P(),
        P(),
        P(),
        P("sub", "pts"),
    )
    out_specs = (P("member", "sub", "pts"), P("member"))
    return jax.shard_map(
        functools.partial(body, mesh.shape["pts"], mesh.shape["sub"]),
        mesh=mesh,
        in_specs=in_specs,
        out_specs=out_specs,
        check_vma=False,
    )
```
